32 devices in a mesh: strip: 8 (over z, y), sub: 4 (over x, core).
Axes of the slice: x: 2, y: 2, z: 4, core: 2. Of those that a mesh axis runs over, the one named last changes fastest.
Arguments:
- flow_field: bfloat16 [64, 512, 512], P('strip', None, 'sub'), may hold values from -6 to 6
- wall_source: bfloat16 [64, 512, 512], P('strip', None, 'sub'), may hold values from -1.1953125 to 1.1953125
- strip_rate: float32 [64], P('strip'), may hold values from 0.05 to 0.24
- strip_pos: int32 [64], P('strip'), may hold values from 0 to 63, as said below
- displace: float32 [64, 512], P('strip', 'sub'), may hold values from -6 to 6
- displace_prev: float32 [64, 512], P('strip', 'sub'), may hold values from -6 to 6
- tension_base: float32 [8], P('strip'), may hold values from 0.05 to 0.25
- anchor_seg: int32 [8], P('strip'), may hold values from 0 to 31
- seg_slot: int32 [32], replicated, may hold values from 0 to 31, each once
Outputs:
- flow_out: bfloat16 [64, 512, 512], P('strip', None, 'sub')
- displace_new: float32 [64, 512], P('strip', 'sub')
- deck_load: float32 [32, 512], P('strip', 'sub')
The draws below stay inside these ranges and needn't reach their ends.
Inputs may be any that keep to these rules, and one draw needn't show every extreme that they name: `strip_pos`: a permutation of the 64 positions; the strips of one index of strip that belong to cables of one owner (position // 8) number 0 or exactly 2.
All inputs are finite; a program needn't handle non-finite values.
Results may differ from the reference program's by a relative error of at most 0.001.
Values may be sent and summed in bfloat16 or wider, within the bound.
A program may use at most 64 MiB of HBM per device.

```python
import math
import jax
import jax.numpy as jnp
import numpy as np
from jax import lax

G = 512
W = 512
SPC = 8
SWEEPS = 8
STRIP_DEV = 8
CAP = 2
S = 64
C = 8
DS = 32
N_STRIP = 8


def draw_strip_pos(key, part):
    slot_groups = STRIP_DEV // CAP
    key_group, key_shift, key_order, key_slot = jax.random.split(key, 4)
    group_perm = jax.random.permutation(key_group, N_STRIP)
    shifts = jax.random.permutation(key_shift, N_STRIP)[:slot_groups]
    orders = jax.vmap(lambda single: jax.random.permutation(single, STRIP_DEV))(jax.random.split(key_order, N_STRIP))
    shift_pick = orders % slot_groups
    copy_pick = orders // slot_groups
    owner_of = (group_perm[:, None] + shifts[shift_pick]) % N_STRIP
    incoming = shift_pick * CAP + copy_pick
    slot_perm = jax.vmap(lambda single: jax.random.permutation(single, STRIP_DEV))(jax.random.split(key_slot, N_STRIP))
    slot_index = slot_perm[owner_of, incoming]
    return (owner_of * STRIP_DEV + slot_index).reshape(-1).astype(jnp.int32)


def place_ends(array, own_key, smallest, high):
    shape = array.shape
    place = [jax.random.randint(jax.random.fold_in(own_key, axis), (), 0, shape[axis]) for axis in range(len(shape))]
    array = array.at[tuple(place)].set(smallest)
    longest = shape.index(max(shape))
    place[longest] = (place[longest] + 1) % shape[longest]
    return array.at[tuple(place)].set(high)


def levels(own_key, dims, cuts, least, top_value):
    gain = 1.0
    for dim, parts in cuts:
        draws = jax.random.uniform(jax.random.fold_in(jax.random.fold_in(own_key, 6), dim), (parts,), jnp.float32, least / len(cuts), top_value / len(cuts))
        gain = gain * jnp.repeat(jnp.exp(draws), dims[dim] // parts).reshape((-1,) + (1,) * (len(dims) - 1 - dim))
    return gain


def rank_bounds(count, slope):
    portions = [(1 << 20) // math.isqrt(standing ** slope) + 1 for standing in range(1, count + 1)]
    width = 1 + sum(portions) // (1 << 30)
    return np.cumsum(np.array([max(1, weight // width) for weight in portions]))


def skewed_ids(key, dims, number_of, skew):
    table = rank_bounds(number_of, skew)
    ticket = jax.random.randint(jax.random.fold_in(key, 1), dims, 0, int(table[number_of - 1]))
    rank = jnp.searchsorted(jnp.asarray(table, jnp.int32), ticket, side="right")
    return jax.random.permutation(jax.random.fold_in(key, 2), number_of)[rank].astype(jnp.int32)


def noise(own_key, extent, spread, bound, pieces=(), dtype=jnp.bfloat16):
    result = spread * jax.random.normal(own_key, extent, jnp.float32)
    if pieces:
        result = result * levels(own_key, extent, pieces, -0.22, 0.18)
    return jnp.clip(result, -bound, bound).astype(dtype)


def setup_inputs(seed: int = 0) -> dict:
    streams_of = jax.random.split(jax.random.key(seed), 10)
    flow_field = noise(streams_of[0], (S, G, W), 1.0, 6.0, ((0, 8), (2, 4)))
    wall_source = noise(streams_of[1], (S, G, W), 0.2, 1.1953125, ((0, 8), (2, 4)))
    strip_rate = jnp.clip(jnp.exp(math.log(0.24) - 1.5686159 * jax.random.uniform(streams_of[2], (S,), jnp.float32) ** levels(streams_of[2], (S,), ((0, 8),), -0.2, 0.2)), 0.05, 0.24)
    strip_pos = draw_strip_pos(jax.random.fold_in(streams_of[9], 71), 0)
    displace = noise(streams_of[4], (S, W), 1.0, 6.0, ((0, 8), (1, 4)), jnp.float32)
    displace_prev = noise(streams_of[5], (S, W), 1.0, 6.0, ((0, 8), (1, 4)), jnp.float32)
    tension_base = jnp.clip(jnp.exp(math.log(0.25) - 1.609438 * jax.random.uniform(streams_of[6], (C,), jnp.float32) ** levels(streams_of[6], (C,), ((0, 8),), -0.2, 0.2)), 0.05, 0.25)
    anchor_seg = place_ends(skewed_ids(streams_of[7], (C,), DS, 2), jax.random.fold_in(streams_of[7], 3), 0, DS - 1).astype(jnp.int32)
    seg_slot = jax.random.permutation(streams_of[8], DS).astype(jnp.int32)
    return dict(flow_field=flow_field, wall_source=wall_source, strip_rate=strip_rate, strip_pos=strip_pos, displace=displace, displace_prev=displace_prev, tension_base=tension_base, anchor_seg=anchor_seg, seg_slot=seg_slot)


def relax_once(values, source_cells, rate_cells):
    padded = jnp.pad(values, ((0, 0), (1, 1), (1, 1)))
    laplace = padded[:, 2:, 1:-1] + padded[:, :-2, 1:-1] + padded[:, 1:-1, 2:] + padded[:, 1:-1, :-2] - 4.0 * values
    return values + rate_cells * laplace + source_cells

def run_group(inputs):
    flow_block, source_block, rate_block = inputs
    values = flow_block.astype(jnp.float32)
    source_cells = source_block.astype(jnp.float32)
    rate_cells = rate_block[:, None, None]
    for sweep_index in range(SWEEPS):
        values = relax_once(values, source_cells, rate_cells)
    force_rows = (lax.optimization_barrier(jnp.sum(values, axis=1)) * (1.0 / math.sqrt(G))).astype(jnp.bfloat16)
    return (values.astype(jnp.bfloat16), force_rows)

def cable_update(positions, previous, force_cells, tension_base):
    extended = jnp.pad(positions, ((0, 0), (1, 1), (0, 0)))
    slopes = extended[:, 1:] - extended[:, :-1]
    stretch = lax.optimization_barrier(jnp.mean(slopes * slopes, axis=1))
    tension = tension_base[:, None] * (1.0 + stretch)
    bending = extended[:, 2:] - 2.0 * positions + extended[:, :-2]
    moved = 2.0 * positions - previous + tension[:, None, :] * bending + 0.5 * force_cells
    return (moved, tension * moved[:, 0, :])

def reference(flow_field, wall_source, strip_rate, strip_pos, displace, displace_prev, tension_base, anchor_seg, seg_slot):
    flow_groups, force_groups = lax.map(run_group, (flow_field.reshape(N_STRIP, STRIP_DEV, G, W), wall_source.reshape(N_STRIP, STRIP_DEV, G, W), strip_rate.reshape(N_STRIP, STRIP_DEV)))
    flow_out = flow_groups.reshape(S, G, W)
    force_rows = force_groups.reshape(S, W)
    cable_force = jnp.zeros((S, W), jnp.bfloat16).at[strip_pos].set(force_rows)
    moved, anchor_rows = cable_update(displace.reshape(C, SPC, W), displace_prev.reshape(C, SPC, W), cable_force.reshape(C, SPC, W).astype(jnp.float32), tension_base)
    target_rows = seg_slot[anchor_seg]
    deck_load = jnp.zeros((DS, W), jnp.float32).at[target_rows].add(anchor_rows)
    return (flow_out, moved.reshape(S, W), deck_load)
```

```python
import functools
import math

import jax
import jax.numpy as jnp
from jax import lax
from jax.experimental import pallas as pl
from jax.experimental.pallas import tpu as pltpu
from jax.sharding import PartitionSpec as P

SWEEPS = 8
HALO = SWEEPS
LANES = 128
SUBL = 8
CHUNK = 16
MESH = pl.DeviceIdType.MESH
F32 = jnp.float32


def kernel(
    n_strip,
    n_sub,
    flow_ref,
    wall_ref,
    rate_ref,
    pos_ref,
    disp_ref,
    prev_ref,
    tens_ref,
    anchor_ref,
    slot_ref,
    out_ref,
    moved_ref,
    deck_ref,
    even,
    odd,
    source,
    staging,
    halo_out,
    halo_in,
    placed,
    placed_in,
    loads,
    loads_in,
    halo_send,
    halo_recv,
    place_send,
    place_recv,
    load_send,
    load_recv,
):
    strips, grid_rows, width = flow_ref.shape
    parts = grid_rows // LANES
    step = parts * strips
    first = HALO * step
    me = lax.axis_index("strip")
    sub = lax.axis_index("sub")
    left = lax.rem(sub + n_sub - 1, n_sub)
    right = lax.rem(sub + 1, n_sub)

    barrier = pltpu.get_barrier_semaphore()
    for neighbour in (left, right):
        pl.semaphore_signal(barrier, inc=1, device_id={"sub": neighbour}, device_id_type=MESH)
    for delta in range(1, n_strip):
        pl.semaphore_signal(
            barrier, inc=1, device_id={"strip": lax.rem(me + delta, n_strip)}, device_id_type=MESH
        )

    lane = lax.broadcasted_iota(jnp.int32, (SUBL, LANES), 1)
    subl = lax.broadcasted_iota(jnp.int32, (SUBL, LANES), 0)
    zero = jnp.zeros((SUBL, LANES), F32)

    for index, (array, target) in enumerate(((flow_ref, even), (wall_ref, source))):
        for strip in range(strips):
            stage = (index * strips + strip) % 2
            staging[stage] = array[strip].astype(F32)
            for part in range(parts):
                block = staging[stage, pl.ds(part, LANES, stride=parts), :]
                target[pl.ds(first + part * strips + strip, width, stride=step), :] = block.T

    rows = HALO * step
    last = first + (width - HALO) * step
    for side, start in ((0, first), (1, last)):
        halo_out[side, 0:rows] = even[start : start + rows].astype(jnp.bfloat16)
        halo_out[side, rows : 2 * rows] = source[start : start + rows].astype(jnp.bfloat16)
    pl.semaphore_wait(barrier, n_strip - 1 + 2)
    halos = []
    for side, neighbour in ((0, left), (1, right)):
        copy = pltpu.make_async_remote_copy(
            src_ref=halo_out.at[side],
            dst_ref=halo_in.at[1 - side],
            send_sem=halo_send.at[side],
            recv_sem=halo_recv.at[1 - side],
            device_id={"sub": neighbour},
            device_id_type=MESH,
        )
        copy.start()
        halos.append(copy)

    rate = zero
    for strip in range(strips):
        rate = jnp.where(subl == strip, rate_ref[strip], rate)
    keep = 1.0 - 4.0 * rate
    has_left = jnp.where(sub > 0, 1.0, 0.0).astype(F32)
    has_right = jnp.where(sub < n_sub - 1, 1.0, 0.0).astype(F32)
    rate_left, rate_right = rate * has_left, rate * has_right
    keep_left, keep_right = 1.0 - 4.0 * rate_left, 1.0 - 4.0 * rate_right
    at_top, at_bottom = lane == 0, lane == LANES - 1

    def relax(old, new, start, columns, factors):
        def cells(ref, column):
            return [
                ref[pl.ds(start + column * step + part * strips, strips), :]
                for part in range(parts)
            ]

        before, here = cells(old, -1), cells(old, 0)
        for u in range(columns):
            after = cells(old, u + 1)
            walls = cells(source, u)
            scale, weight = factors(u)
            for part in range(parts):
                if part > 0:
                    up = here[part - 1]
                else:
                    up = jnp.where(at_top, 0.0, pltpu.roll(here[parts - 1], 1, 1))
                if part < parts - 1:
                    down = here[part + 1]
                else:
                    down = jnp.where(at_bottom, 0.0, pltpu.roll(here[0], LANES - 1, 1))
                around = (before[part] + after[part]) + (up + down)
                new[pl.ds(start + u * step + part * strips, strips), :] = (
                    scale * here[part] + walls[part]
                ) + weight * around
            before, here = here, after

    inner = lambda u: (keep, rate)
    buffers = (even, odd)

    chunks = (width - 2 * HALO) // CHUNK
    for sweep in range(1, SWEEPS + 1):
        old, new = buffers[(sweep - 1) % 2], buffers[sweep % 2]

        def body(chunk, carry, old=old, new=new):
            start = pl.multiple_of(2 * first + chunk * (CHUNK * step), CHUNK * step)
            relax(old, new, start, CHUNK, inner)
            return carry

        lax.fori_loop(0, chunks, body, 0)
        side = HALO - sweep
        if side:
            relax(old, new, first + sweep * step, side, inner)
            relax(old, new, first + (width - HALO) * step, side, inner)

    for copy in halos:
        copy.wait()
    for side, start, mask in ((0, 0, has_left), (1, first + width * step, has_right)):
        even[start : start + rows] = halo_in[side, 0:rows].astype(F32) * mask
        source[start : start + rows] = halo_in[side, rows : 2 * rows].astype(F32) * mask
    for sweep in range(1, SWEEPS + 1):
        old, new = buffers[(sweep - 1) % 2], buffers[sweep % 2]
        relax(
            old,
            new,
            sweep * step,
            HALO,
            lambda u: (keep_left, rate_left) if u + sweep < HALO else (keep, rate),
        )
        relax(
            old,
            new,
            first + (width - sweep) * step,
            HALO,
            lambda u: (keep_right, rate_right) if u >= sweep else (keep, rate),
        )
    final = buffers[SWEEPS % 2]

    force = []
    for strip in range(strips):
        total = None
        for part in range(parts):
            block = final[pl.ds(first + part * strips + strip, width, stride=step), :]
            total = block if total is None else total + block
        row = jnp.sum(total.T, axis=0, keepdims=True) * (1.0 / math.sqrt(grid_rows))
        force.append(row.astype(jnp.bfloat16).astype(F32))
    for owner in range(n_strip):
        tile = zero
        for strip in range(strips):
            tile = tile + jnp.where(subl + owner * strips == pos_ref[strip], force[strip], 0.0)
        placed[owner] = tile

    def exchange(tiles, landing, send_sems, recv_sems):
        copies = []
        for delta in range(1, n_strip):
            target = lax.rem(me + delta, n_strip)
            copy = pltpu.make_async_remote_copy(
                src_ref=tiles.at[target],
                dst_ref=landing.at[delta],
                send_sem=send_sems.at[delta],
                recv_sem=recv_sems.at[delta],
                device_id={"strip": target},
                device_id_type=MESH,
            )
            copy.start()
            copies.append(copy)
        return copies

    copies = exchange(placed, placed_in, place_send, place_recv)

    for strip in range(strips):
        stage = strip % 2
        for part in range(parts):
            block = final[pl.ds(first + part * strips + strip, width, stride=step), :]
            staging[stage, pl.ds(part, LANES, stride=parts), :] = block.T
        out_ref[strip] = staging[stage].astype(jnp.bfloat16)

    u = disp_ref[...]
    above = jnp.where(subl == 0, 0.0, pltpu.roll(u, 1, 0))
    below = jnp.where(subl == SUBL - 1, 0.0, pltpu.roll(u, SUBL - 1, 0))
    slope = u - above
    squares = slope * slope + jnp.where(subl == SUBL - 1, u * u, 0.0)
    stretch = jnp.sum(squares, axis=0, keepdims=True) * (1.0 / (SUBL + 1))
    tension = tens_ref[0] * (1.0 + stretch)
    moved = 2.0 * u - prev_ref[...] + tension * (below - 2.0 * u + above)

    cable_force = placed[me]
    for delta, copy in enumerate(copies, 1):
        copy.wait()
        cable_force = cable_force + placed_in[delta]
    moved = moved + 0.5 * cable_force
    moved_ref[...] = moved
    anchor = tension * moved[0:1, :]

    deck_rows = deck_ref.shape[0]
    wanted = slot_ref[anchor_ref[0]]
    for owner in range(n_strip):
        hit = (subl + owner * deck_rows == wanted) & (subl < deck_rows)
        loads[owner] = jnp.where(hit, anchor, 0.0)
    copies = exchange(loads, loads_in, load_send, load_recv)
    total = loads[me]
    for delta, copy in enumerate(copies, 1):
        copy.wait()
        total = total + loads_in[delta]
    deck_ref[...] = total[0:deck_rows, :]


def per_device(n_strip, n_sub, *args):
    flow_field, _, _, _, displace = args[:5]
    seg_slot = args[8]
    strips, grid_rows, width = flow_field.shape
    step = grid_rows // LANES * strips
    rows = (width + 2 * HALO) * step
    deck_rows = seg_slot.shape[0] // n_strip
    vmem = pl.BlockSpec(memory_space=pltpu.VMEM)
    smem = pl.BlockSpec(memory_space=pltpu.SMEM)
    dma = pltpu.SemaphoreType.DMA
    return pl.pallas_call(
        functools.partial(kernel, n_strip, n_sub),
        out_shape=(
            jax.ShapeDtypeStruct(flow_field.shape, jnp.bfloat16),
            jax.ShapeDtypeStruct(displace.shape, F32),
            jax.ShapeDtypeStruct((deck_rows, width), F32),
        ),
        in_specs=[vmem, vmem, smem, smem, vmem, vmem, smem, smem, smem],
        out_specs=(vmem, vmem, vmem),
        scratch_shapes=[
            pltpu.VMEM((rows, LANES), F32),
            pltpu.VMEM((rows, LANES), F32),
            pltpu.VMEM((rows, LANES), F32),
            pltpu.VMEM((2, grid_rows, LANES), F32),
            pltpu.VMEM((2, 2 * HALO * step, LANES), jnp.bfloat16),
            pltpu.VMEM((2, 2 * HALO * step, LANES), jnp.bfloat16),
            pltpu.VMEM((n_strip, SUBL, LANES), F32),
            pltpu.VMEM((n_strip, SUBL, LANES), F32),
            pltpu.VMEM((n_strip, SUBL, LANES), F32),
            pltpu.VMEM((n_strip, SUBL, LANES), F32),
            dma((2,)),
            dma((2,)),
            dma((n_strip,)),
            dma((n_strip,)),
            dma((n_strip,)),
            dma((n_strip,)),
        ],
        compiler_params=pltpu.CompilerParams(
            collective_id=0, has_side_effects=True, vmem_limit_bytes=32 * 1024 * 1024
        ),
    )(*args)


def solution(mesh):
    in_specs = (
        P("strip", None, "sub"),
        P("strip", None, "sub"),
        P("strip"),
        P("strip"),
        P("strip", "sub"),
        P("strip", "sub"),
        P("strip"),
        P("strip"),
        P(),
    )
    out_specs = (P("strip", None, "sub"), P("strip", "sub"), P("strip", "sub"))
    return jax.shard_map(
        functools.partial(per_device, mesh.shape["strip"], mesh.shape["sub"]),
        mesh=mesh,
        in_specs=in_specs,
        out_specs=out_specs,
        check_vma=False,
    )
```

```python
import functools
import math

import jax
import jax.numpy as jnp
from jax import lax
from jax.experimental import pallas as pl
from jax.experimental.pallas import tpu as pltpu
from jax.sharding import PartitionSpec as P

SWEEPS = 8
HALO = SWEEPS
LANES = 128
SUBL = 8
CHUNK = 28
MESH = pl.DeviceIdType.MESH
F32 = jnp.float32


def kernel(
    n_strip,
    n_sub,
    flow_hbm,
    wall_hbm,
    rate_ref,
    pos_ref,
    disp_hbm,
    prev_hbm,
    tens_ref,
    anchor_ref,
    slot_ref,
    out_hbm,
    moved_ref,
    deck_ref,
    even,
    odd,
    source,
    staging,
    halo_out,
    halo_in,
    tiles,
    tiles_in,
    info,
    info_in,
    flow_ref,
    wall_ref,
    disp_ref,
    prev_ref,
    out_ref,
    halo_send,
    halo_recv,
    tile_send,
    tile_recv,
    info_send,
    info_recv,
    in_sem,
    small_sem,
    out_sem,
):
    strips, grid_rows, width = flow_ref.shape
    arriving = [
        [
            pltpu.make_async_copy(array.at[strip], target.at[strip], in_sem.at[index, strip])
            for strip in range(strips)
        ]
        for index, (array, target) in enumerate(((flow_hbm, flow_ref), (wall_hbm, wall_ref)))
    ]
    small = [
        pltpu.make_async_copy(array, target, small_sem.at[index])
        for index, (array, target) in enumerate(((disp_hbm, disp_ref), (prev_hbm, prev_ref)))
    ]
    for copy in small + arriving[0] + arriving[1]:
        copy.start()
    parts = grid_rows // LANES
    step = parts * strips
    first = HALO * step
    me = lax.axis_index("strip")
    sub = lax.axis_index("sub")
    left = lax.rem(sub + n_sub - 1, n_sub)
    right = lax.rem(sub + 1, n_sub)

    barrier = pltpu.get_barrier_semaphore()
    for neighbour in (left, right):
        pl.semaphore_signal(barrier, inc=1, device_id={"sub": neighbour}, device_id_type=MESH)
    for delta in range(1, n_strip):
        pl.semaphore_signal(
            barrier, inc=1, device_id={"strip": lax.rem(me + delta, n_strip)}, device_id_type=MESH
        )

    lane = lax.broadcasted_iota(jnp.int32, (SUBL, LANES), 1)
    subl = lax.broadcasted_iota(jnp.int32, (SUBL, LANES), 0)
    zero = jnp.zeros((SUBL, LANES), F32)

    for index, (array, target) in enumerate(((flow_ref, even), (wall_ref, source))):
        for strip in range(strips):
            stage = (index * strips + strip) % 2
            arriving[index][strip].wait()
            staging[stage] = array[strip].astype(F32)
            for part in range(parts):
                block = staging[stage, pl.ds(part, LANES, stride=parts), :]
                target[pl.ds(first + part * strips + strip, width, stride=step), :] = block.T

    rows = HALO * step
    last = first + (width - HALO) * step
    for side, start in ((0, first), (1, last)):
        halo_out[side, 0:rows] = even[start : start + rows].astype(jnp.bfloat16)
        halo_out[side, rows : 2 * rows] = source[start : start + rows].astype(jnp.bfloat16)
    pl.semaphore_wait(barrier, n_strip - 1 + 2)
    halos = []
    for side, neighbour in ((0, left), (1, right)):
        copy = pltpu.make_async_remote_copy(
            src_ref=halo_out.at[side],
            dst_ref=halo_in.at[1 - side],
            send_sem=halo_send.at[side],
            recv_sem=halo_recv.at[1 - side],
            device_id={"sub": neighbour},
            device_id_type=MESH,
        )
        copy.start()
        halos.append(copy)

    for copy in small:
        copy.wait()
    u = disp_ref[...]
    above = jnp.where(subl == 0, 0.0, pltpu.roll(u, 1, 0))
    below = jnp.where(subl == SUBL - 1, 0.0, pltpu.roll(u, SUBL - 1, 0))
    slope = u - above
    squares = slope * slope + jnp.where(subl == SUBL - 1, u * u, 0.0)
    stretch = jnp.sum(squares, axis=0, keepdims=True) * (1.0 / (SUBL + 1))
    tension = tens_ref[0] * (1.0 + stretch)
    moved = 2.0 * u - prev_ref[...] + tension * (below - 2.0 * u + above)

    wanted = slot_ref[anchor_ref[0]].astype(F32)
    info[0:1, :] = tension
    info[1:2, :] = tension * moved[0:1, :]
    info[2:SUBL, :] = jnp.full((SUBL - 2, LANES), wanted, F32)

    def exchange(source_of, landing, send_sems, recv_sems):
        copies = []
        for delta in range(1, n_strip):
            target = lax.rem(me + delta, n_strip)
            copy = pltpu.make_async_remote_copy(
                src_ref=source_of(target),
                dst_ref=landing.at[delta],
                send_sem=send_sems.at[delta],
                recv_sem=recv_sems.at[delta],
                device_id={"strip": target},
                device_id_type=MESH,
            )
            copy.start()
            copies.append(copy)
        return copies

    sent = exchange(lambda target: info, info_in, info_send, info_recv)

    rate = zero
    for strip in range(strips):
        rate = jnp.where(subl == strip, rate_ref[strip], rate)
    keep = 1.0 - 4.0 * rate
    has_left = jnp.where(sub > 0, 1.0, 0.0).astype(F32)
    has_right = jnp.where(sub < n_sub - 1, 1.0, 0.0).astype(F32)
    rate_left, rate_right = rate * has_left, rate * has_right
    keep_left, keep_right = 1.0 - 4.0 * rate_left, 1.0 - 4.0 * rate_right
    at_top, at_bottom = lane == 0, lane == LANES - 1

    def relax(old, new, start, columns, factors):
        def cells(ref, column):
            return [
                ref[pl.ds(start + column * step + part * strips, strips), :]
                for part in range(parts)
            ]

        before, here = cells(old, -1), cells(old, 0)
        for u in range(columns):
            after = cells(old, u + 1)
            walls = cells(source, u)
            scale, weight = factors(u)
            for part in range(parts):
                if part > 0:
                    up = here[part - 1]
                else:
                    up = jnp.where(at_top, 0.0, pltpu.roll(here[parts - 1], 1, 1))
                if part < parts - 1:
                    down = here[part + 1]
                else:
                    down = jnp.where(at_bottom, 0.0, pltpu.roll(here[0], LANES - 1, 1))
                around = (before[part] + after[part]) + (up + down)
                new[pl.ds(start + u * step + part * strips, strips), :] = (
                    scale * here[part] + walls[part]
                ) + weight * around
            before, here = here, after

    inner = lambda u: (keep, rate)
    buffers = (even, odd)

    chunks = (width - 2 * HALO) // CHUNK
    for sweep in range(1, SWEEPS + 1):
        old, new = buffers[(sweep - 1) % 2], buffers[sweep % 2]

        def body(chunk, carry, old=old, new=new):
            start = pl.multiple_of(2 * first + chunk * (CHUNK * step), 4 * step)
            relax(old, new, start, CHUNK, inner)
            return carry

        lax.fori_loop(0, chunks, body, 0)
        side = HALO - sweep
        if side:
            relax(old, new, first + sweep * step, side, inner)
            relax(old, new, first + (width - HALO) * step, side, inner)

    for copy in halos:
        copy.wait()
    for side, start, mask in ((0, 0, has_left), (1, first + width * step, has_right)):
        even[start : start + rows] = halo_in[side, 0:rows].astype(F32) * mask
        source[start : start + rows] = halo_in[side, rows : 2 * rows].astype(F32) * mask
    for sweep in range(1, SWEEPS + 1):
        old, new = buffers[(sweep - 1) % 2], buffers[sweep % 2]
        relax(
            old,
            new,
            sweep * step,
            HALO,
            lambda u: (keep_left, rate_left) if u + sweep < HALO else (keep, rate),
        )
        relax(
            old,
            new,
            first + (width - sweep) * step,
            HALO,
            lambda u: (keep_right, rate_right) if u >= sweep else (keep, rate),
        )
    final = buffers[SWEEPS % 2]

    force = []
    for strip in range(strips):
        total = None
        for part in range(parts):
            block = final[pl.ds(first + part * strips + strip, width, stride=step), :]
            total = block if total is None else total + block
        row = jnp.sum(total.T, axis=0, keepdims=True) * (1.0 / math.sqrt(grid_rows))
        force.append(row.astype(jnp.bfloat16).astype(F32))
    for owner in range(n_strip):
        tile = zero
        for strip in range(strips):
            tile = tile + jnp.where(subl + owner * strips == pos_ref[strip], force[strip], 0.0)
        tiles[owner, 0:SUBL] = tile

    for copy in sent:
        copy.wait()
    deck_rows = deck_ref.shape[0]
    subf = jnp.where(subl < deck_rows, subl, -(2**20)).astype(F32)
    cables = []
    for delta in range(n_strip):
        told = info if delta == 0 else info_in.at[delta]
        at_first = tiles[lax.rem(me + n_strip - delta, n_strip), 0:1]
        row, base = told[2:3, :], told[1:2, :]
        cables.append((row, base, 0.5 * told[0:1, :] * at_first))
    for owner in range(n_strip):
        tile = zero
        for row, base, share in cables:
            tile = tile + jnp.where(subf + float(owner * deck_rows) == row, share, 0.0)
        tiles[owner, SUBL : 2 * SUBL] = tile

    copies = exchange(lambda target: tiles.at[target], tiles_in, tile_send, tile_recv)

    mine = (me * deck_rows).astype(F32)
    total = zero
    for row, base, share in cables:
        total = total + jnp.where(subf + mine == row, base, 0.0)

    leaving = []
    for strip in range(strips):
        stage = strip % 2
        for part in range(parts):
            block = final[pl.ds(first + part * strips + strip, width, stride=step), :]
            staging[stage, pl.ds(part, LANES, stride=parts), :] = block.T
        out_ref[strip] = staging[stage].astype(jnp.bfloat16)
        copy = pltpu.make_async_copy(out_ref.at[strip], out_hbm.at[strip], out_sem.at[strip])
        copy.start()
        leaving.append(copy)

    cable_force = tiles[me, 0:SUBL]
    total = total + tiles[me, SUBL : 2 * SUBL]
    for delta, copy in enumerate(copies, 1):
        copy.wait()
        cable_force = cable_force + tiles_in[delta, 0:SUBL]
        total = total + tiles_in[delta, SUBL : 2 * SUBL]
    moved_ref[...] = moved + 0.5 * cable_force
    deck_ref[...] = total[0:deck_rows, :]
    for copy in leaving:
        copy.wait()


def per_device(n_strip, n_sub, *args):
    flow_field, _, _, _, displace = args[:5]
    seg_slot = args[8]
    strips, grid_rows, width = flow_field.shape
    step = grid_rows // LANES * strips
    rows = (width + 2 * HALO) * step
    deck_rows = seg_slot.shape[0] // n_strip
    vmem = pl.BlockSpec(memory_space=pltpu.VMEM)
    anywhere = pl.BlockSpec(memory_space=pl.ANY)
    smem = pl.BlockSpec(memory_space=pltpu.SMEM)
    dma = pltpu.SemaphoreType.DMA
    return pl.pallas_call(
        functools.partial(kernel, n_strip, n_sub),
        out_shape=(
            jax.ShapeDtypeStruct(flow_field.shape, jnp.bfloat16),
            jax.ShapeDtypeStruct(displace.shape, F32),
            jax.ShapeDtypeStruct((deck_rows, width), F32),
        ),
        in_specs=[anywhere, anywhere, smem, smem, anywhere, anywhere, smem, smem, smem],
        out_specs=(anywhere, vmem, vmem),
        scratch_shapes=[
            pltpu.VMEM((rows, LANES), F32),
            pltpu.VMEM((rows, LANES), F32),
            pltpu.VMEM((rows, LANES), F32),
            pltpu.VMEM((2, grid_rows, LANES), F32),
            pltpu.VMEM((2, 2 * HALO * step, LANES), jnp.bfloat16),
            pltpu.VMEM((2, 2 * HALO * step, LANES), jnp.bfloat16),
            pltpu.VMEM((n_strip, 2 * SUBL, LANES), F32),
            pltpu.VMEM((n_strip, 2 * SUBL, LANES), F32),
            pltpu.VMEM((SUBL, LANES), F32),
            pltpu.VMEM((n_strip, SUBL, LANES), F32),
            pltpu.VMEM(flow_field.shape, jnp.bfloat16),
            pltpu.VMEM(flow_field.shape, jnp.bfloat16),
            pltpu.VMEM(displace.shape, F32),
            pltpu.VMEM(displace.shape, F32),
            pltpu.VMEM(flow_field.shape, jnp.bfloat16),
            dma((2,)),
            dma((2,)),
            dma((n_strip,)),
            dma((n_strip,)),
            dma((n_strip,)),
            dma((n_strip,)),
            dma((2, strips)),
            dma((2,)),
            dma((strips,)),
        ],
        compiler_params=pltpu.CompilerParams(
            collective_id=0, has_side_effects=True, vmem_limit_bytes=56 * 1024 * 1024
        ),
    )(*args)


def solution(mesh):
    in_specs = (
        P("strip", None, "sub"),
        P("strip", None, "sub"),
        P("strip"),
        P("strip"),
        P("strip", "sub"),
        P("strip", "sub"),
        P("strip"),
        P("strip"),
        P(),
    )
    out_specs = (P("strip", None, "sub"), P("strip", "sub"), P("strip", "sub"))
    return jax.shard_map(
        functools.partial(per_device, mesh.shape["strip"], mesh.shape["sub"]),
        mesh=mesh,
        in_specs=in_specs,
        out_specs=out_specs,
        check_vma=False,
    )
```

```python
import functools
import math

import jax
import jax.numpy as jnp
from jax import lax
from jax.experimental import pallas as pl
from jax.experimental.pallas import tpu as pltpu
from jax.sharding import PartitionSpec as P

SWEEPS = 8
HALO = SWEEPS
LANES = 128
SUBL = 8
CHUNK = 56
MESH = pl.DeviceIdType.MESH
F32 = jnp.float32


def kernel(
    n_strip,
    n_sub,
    flow_hbm,
    wall_hbm,
    rate_ref,
    pos_ref,
    disp_hbm,
    prev_hbm,
    tens_ref,
    anchor_ref,
    slot_ref,
    out_hbm,
    moved_ref,
    deck_ref,
    even,
    odd,
    source,
    staging,
    halo_out,
    halo_in,
    tiles,
    tiles_in,
    info,
    info_in,
    flow_ref,
    wall_ref,
    disp_ref,
    prev_ref,
    out_ref,
    halo_send,
    halo_recv,
    tile_send,
    tile_recv,
    info_send,
    info_recv,
    in_sem,
    small_sem,
    out_sem,
):
    strips, grid_rows, width = flow_ref.shape
    arriving = [
        [
            pltpu.make_async_copy(array.at[strip], target.at[strip], in_sem.at[index, strip])
            for strip in range(strips)
        ]
        for index, (array, target) in enumerate(((flow_hbm, flow_ref), (wall_hbm, wall_ref)))
    ]
    small = [
        pltpu.make_async_copy(array, target, small_sem.at[index])
        for index, (array, target) in enumerate(((disp_hbm, disp_ref), (prev_hbm, prev_ref)))
    ]
    for copy in small + arriving[0] + arriving[1]:
        copy.start()
    parts = grid_rows // LANES
    step = parts * strips
    first = HALO * step
    me = lax.axis_index("strip")
    sub = lax.axis_index("sub")
    left = lax.rem(sub + n_sub - 1, n_sub)
    right = lax.rem(sub + 1, n_sub)

    barrier = pltpu.get_barrier_semaphore()
    for neighbour in (left, right):
        pl.semaphore_signal(barrier, inc=1, device_id={"sub": neighbour}, device_id_type=MESH)
    for delta in range(1, n_strip):
        pl.semaphore_signal(
            barrier, inc=1, device_id={"strip": lax.rem(me + delta, n_strip)}, device_id_type=MESH
        )

    lane = lax.broadcasted_iota(jnp.int32, (SUBL, LANES), 1)
    subl = lax.broadcasted_iota(jnp.int32, (SUBL, LANES), 0)
    zero = jnp.zeros((SUBL, LANES), F32)

    for index, (array, target) in enumerate(((flow_ref, even), (wall_ref, source))):
        for strip in range(strips):
            stage = (index * strips + strip) % 2
            arriving[index][strip].wait()
            staging[stage] = array[strip].astype(F32)
            for part in range(parts):
                block = staging[stage, pl.ds(part, LANES, stride=parts), :]
                target[pl.ds(first + part * strips + strip, width, stride=step), :] = block.T

    rows = HALO * step
    last = first + (width - HALO) * step
    for side, start in ((0, first), (1, last)):
        halo_out[side, 0:rows] = even[start : start + rows].astype(jnp.bfloat16)
        halo_out[side, rows : 2 * rows] = source[start : start + rows].astype(jnp.bfloat16)
    pl.semaphore_wait(barrier, n_strip - 1 + 2)
    halos = []
    for side, neighbour in ((0, left), (1, right)):
        copy = pltpu.make_async_remote_copy(
            src_ref=halo_out.at[side],
            dst_ref=halo_in.at[1 - side],
            send_sem=halo_send.at[side],
            recv_sem=halo_recv.at[1 - side],
            device_id={"sub": neighbour},
            device_id_type=MESH,
        )
        copy.start()
        halos.append(copy)

    for copy in small:
        copy.wait()
    u = disp_ref[...]
    above = jnp.where(subl == 0, 0.0, pltpu.roll(u, 1, 0))
    below = jnp.where(subl == SUBL - 1, 0.0, pltpu.roll(u, SUBL - 1, 0))
    slope = u - above
    squares = slope * slope + jnp.where(subl == SUBL - 1, u * u, 0.0)
    stretch = jnp.sum(squares, axis=0, keepdims=True) * (1.0 / (SUBL + 1))
    tension = tens_ref[0] * (1.0 + stretch)
    moved = 2.0 * u - prev_ref[...] + tension * (below - 2.0 * u + above)

    wanted = slot_ref[anchor_ref[0]].astype(F32)
    info[0:1, :] = tension
    info[1:2, :] = tension * moved[0:1, :]
    info[2:SUBL, :] = jnp.full((SUBL - 2, LANES), wanted, F32)

    def exchange(source_of, landing, send_sems, recv_sems):
        copies = []
        for delta in range(1, n_strip):
            target = lax.rem(me + delta, n_strip)
            copy = pltpu.make_async_remote_copy(
                src_ref=source_of(target),
                dst_ref=landing.at[delta],
                send_sem=send_sems.at[delta],
                recv_sem=recv_sems.at[delta],
                device_id={"strip": target},
                device_id_type=MESH,
            )
            copy.start()
            copies.append(copy)
        return copies

    sent = exchange(lambda target: info, info_in, info_send, info_recv)

    rate = zero
    for strip in range(strips):
        rate = jnp.where(subl == strip, rate_ref[strip], rate)
    keep = 1.0 - 4.0 * rate
    has_left = jnp.where(sub > 0, 1.0, 0.0).astype(F32)
    has_right = jnp.where(sub < n_sub - 1, 1.0, 0.0).astype(F32)
    rate_left, rate_right = rate * has_left, rate * has_right
    keep_left, keep_right = 1.0 - 4.0 * rate_left, 1.0 - 4.0 * rate_right
    at_top, at_bottom = lane == 0, lane == LANES - 1

    def relax(old, new, start, columns, factors):
        def cells(ref, column):
            return [
                ref[pl.ds(start + column * step + part * strips, strips), :]
                for part in range(parts)
            ]

        before, here = cells(old, -1), cells(old, 0)
        for u in range(columns):
            after = cells(old, u + 1)
            walls = cells(source, u)
            scale, weight = factors(u)
            for part in range(parts):
                if part > 0:
                    up = here[part - 1]
                else:
                    up = jnp.where(at_top, 0.0, pltpu.roll(here[parts - 1], 1, 1))
                if part < parts - 1:
                    down = here[part + 1]
                else:
                    down = jnp.where(at_bottom, 0.0, pltpu.roll(here[0], LANES - 1, 1))
                around = (before[part] + after[part]) + (up + down)
                new[pl.ds(start + u * step + part * strips, strips), :] = (
                    scale * here[part] + walls[part]
                ) + weight * around
            before, here = here, after

    inner = lambda u: (keep, rate)
    buffers = (even, odd)

    chunks = (width - 2 * HALO) // CHUNK
    for sweep in range(1, SWEEPS + 1):
        old, new = buffers[(sweep - 1) % 2], buffers[sweep % 2]

        def body(chunk, carry, old=old, new=new):
            start = pl.multiple_of(2 * first + chunk * (CHUNK * step), 4 * step)
            relax(old, new, start, CHUNK, inner)
            return carry

        lax.fori_loop(0, chunks, body, 0)
        side = HALO - sweep
        if side:
            relax(old, new, first + sweep * step, side, inner)
            relax(old, new, first + (width - HALO) * step, side, inner)

    for copy in halos:
        copy.wait()
    for side, start, mask in ((0, 0, has_left), (1, first + width * step, has_right)):
        even[start : start + rows] = halo_in[side, 0:rows].astype(F32) * mask
        source[start : start + rows] = halo_in[side, rows : 2 * rows].astype(F32) * mask
    for sweep in range(1, SWEEPS + 1):
        old, new = buffers[(sweep - 1) % 2], buffers[sweep % 2]
        relax(
            old,
            new,
            sweep * step,
            HALO,
            lambda u: (keep_left, rate_left) if u + sweep < HALO else (keep, rate),
        )
        relax(
            old,
            new,
            first + (width - sweep) * step,
            HALO,
            lambda u: (keep_right, rate_right) if u >= sweep else (keep, rate),
        )
    final = buffers[SWEEPS % 2]

    force = []
    for strip in range(strips):
        total = None
        for part in range(parts):
            block = final[pl.ds(first + part * strips + strip, width, stride=step), :]
            total = block if total is None else total + block
        row = jnp.sum(total.T, axis=0, keepdims=True) * (1.0 / math.sqrt(grid_rows))
        force.append(row.astype(jnp.bfloat16).astype(F32))
    for owner in range(n_strip):
        tile = zero
        for strip in range(strips):
            tile = tile + jnp.where(subl + owner * strips == pos_ref[strip], force[strip], 0.0)
        tiles[owner, 0:SUBL] = tile

    for copy in sent:
        copy.wait()
    deck_rows = deck_ref.shape[0]
    subf = jnp.where(subl < deck_rows, subl, -(2**20)).astype(F32)
    cables = []
    for delta in range(n_strip):
        told = info if delta == 0 else info_in.at[delta]
        at_first = tiles[lax.rem(me + n_strip - delta, n_strip), 0:1]
        row, base = told[2:3, :], told[1:2, :]
        cables.append((row, base, 0.5 * told[0:1, :] * at_first))
    for owner in range(n_strip):
        tile = zero
        for row, base, share in cables:
            tile = tile + jnp.where(subf + float(owner * deck_rows) == row, share, 0.0)
        tiles[owner, SUBL : 2 * SUBL] = tile

    copies = exchange(lambda target: tiles.at[target], tiles_in, tile_send, tile_recv)

    mine = (me * deck_rows).astype(F32)
    total = zero
    for row, base, share in cables:
        total = total + jnp.where(subf + mine == row, base, 0.0)

    leaving = []
    for strip in range(strips):
        stage = strip % 2
        for part in range(parts):
            block = final[pl.ds(first + part * strips + strip, width, stride=step), :]
            staging[stage, pl.ds(part, LANES, stride=parts), :] = block.T
        out_ref[strip] = staging[stage].astype(jnp.bfloat16)
        copy = pltpu.make_async_copy(out_ref.at[strip], out_hbm.at[strip], out_sem.at[strip])
        copy.start()
        leaving.append(copy)

    cable_force = tiles[me, 0:SUBL]
    total = total + tiles[me, SUBL : 2 * SUBL]
    for delta, copy in enumerate(copies, 1):
        copy.wait()
        cable_force = cable_force + tiles_in[delta, 0:SUBL]
        total = total + tiles_in[delta, SUBL : 2 * SUBL]
    moved_ref[...] = moved + 0.5 * cable_force
    deck_ref[...] = total[0:deck_rows, :]
    for copy in leaving:
        copy.wait()


def per_device(n_strip, n_sub, *args):
    flow_field, _, _, _, displace = args[:5]
    seg_slot = args[8]
    strips, grid_rows, width = flow_field.shape
    step = grid_rows // LANES * strips
    rows = (width + 2 * HALO) * step
    deck_rows = seg_slot.shape[0] // n_strip
    vmem = pl.BlockSpec(memory_space=pltpu.VMEM)
    anywhere = pl.BlockSpec(memory_space=pl.ANY)
    smem = pl.BlockSpec(memory_space=pltpu.SMEM)
    dma = pltpu.SemaphoreType.DMA
    return pl.pallas_call(
        functools.partial(kernel, n_strip, n_sub),
        out_shape=(
            jax.ShapeDtypeStruct(flow_field.shape, jnp.bfloat16),
            jax.ShapeDtypeStruct(displace.shape, F32),
            jax.ShapeDtypeStruct((deck_rows, width), F32),
        ),
        in_specs=[anywhere, anywhere, smem, smem, anywhere, anywhere, smem, smem, smem],
        out_specs=(anywhere, vmem, vmem),
        scratch_shapes=[
            pltpu.VMEM((rows, LANES), F32),
            pltpu.VMEM((rows, LANES), F32),
            pltpu.VMEM((rows, LANES), F32),
            pltpu.VMEM((2, grid_rows, LANES), F32),
            pltpu.VMEM((2, 2 * HALO * step, LANES), jnp.bfloat16),
            pltpu.VMEM((2, 2 * HALO * step, LANES), jnp.bfloat16),
            pltpu.VMEM((n_strip, 2 * SUBL, LANES), F32),
            pltpu.VMEM((n_strip, 2 * SUBL, LANES), F32),
            pltpu.VMEM((SUBL, LANES), F32),
            pltpu.VMEM((n_strip, SUBL, LANES), F32),
            pltpu.VMEM(flow_field.shape, jnp.bfloat16),
            pltpu.VMEM(flow_field.shape, jnp.bfloat16),
            pltpu.VMEM(displace.shape, F32),
            pltpu.VMEM(displace.shape, F32),
            pltpu.VMEM(flow_field.shape, jnp.bfloat16),
            dma((2,)),
            dma((2,)),
            dma((n_strip,)),
            dma((n_strip,)),
            dma((n_strip,)),
            dma((n_strip,)),
            dma((2, strips)),
            dma((2,)),
            dma((strips,)),
        ],
        compiler_params=pltpu.CompilerParams(
            collective_id=0, has_side_effects=True, vmem_limit_bytes=56 * 1024 * 1024
        ),
    )(*args)


def solution(mesh):
    in_specs = (
        P("strip", None, "sub"),
        P("strip", None, "sub"),
        P("strip"),
        P("strip"),
        P("strip", "sub"),
        P("strip", "sub"),
        P("strip"),
        P("strip"),
        P(),
    )
    out_specs = (P("strip", None, "sub"), P("strip", "sub"), P("strip", "sub"))
    return jax.shard_map(
        functools.partial(per_device, mesh.shape["strip"], mesh.shape["sub"]),
        mesh=mesh,
        in_specs=in_specs,
        out_specs=out_specs,
        check_vma=False,
    )
```
